512 devices in a mesh: wide: 128 (over z, y, core), narrow: 4 (over x).
Axes of the slice: x: 4, y: 8, z: 8, core: 2. Of those that a mesh axis runs over, the one named last changes fastest.
Arguments:
- comps: bfloat16 [1024, 512, 128], P('wide', 'narrow'), may hold values from -6 to 6
- entry: int32 [1024, 512], P('wide', 'narrow'), may hold values from 0 to 15
- dest: int32 [128, 4, 1024, 1], P('wide', 'narrow'), may hold values from 0 to 127; in each aligned block of 1024 rows (0 to 1023, 1024 to 2047, ..., all dimensions but the last counted through in order) at most 12 rows name the same one
- slot_of_entry: int32 [128, 4, 16], P('wide', 'narrow'), may hold values from 0 to 15, each once within a row
- table_f0: bfloat16 [128, 4, 16, 128], P('wide', 'narrow'), may hold values from -6 to 6
- table_x0: bfloat16 [128, 4, 16, 128], P('wide', 'narrow'), may hold values from -6 to 6
- table_a: bfloat16 [128, 4, 16, 128, 128], P('wide', 'narrow'), may hold values from -0.5 to 0.5
- courant_x: float32 [1024, 512], P('wide', 'narrow'), may hold values from -0.4 to 0.4
- courant_y: float32 [1024, 512], P('wide', 'narrow'), may hold values from -0.4 to 0.4
- diffusion: float32 [128], replicated, may hold values from 0.02 to 0.1
Outputs:
- transported: float32 [1024, 512, 128], P('wide', 'narrow')
The draws below stay inside these ranges and needn't reach their ends.
Inputs may be any that keep to these rules, and one draw needn't show every extreme that they name: `dest`: at most 12 cells of one device name the same owner, and exactly 12 do so on some device. `slot_of_entry`: each row is a permutation.
All inputs are finite; a program needn't handle non-finite values.
Results may differ from the reference program's by a relative error of at most 0.0039.
Values may be sent and summed in bfloat16 or wider, within the bound.
A program may use at most 64 MiB of HBM per device.

```python
import math
import jax
import jax.numpy as jnp
import numpy as np
from jax import lax

K = 128
CX = 8
CY = 128
E_LOC = 16
NX = 1024
NY = 512
CAP = 12
N_WIDE = 128
N_NARROW = 4


def place_ends(drawn, key, low, high):
    place = [jax.random.randint(jax.random.fold_in(key, axis), (), 0, length) for axis, length in enumerate(drawn.shape)]
    widest = drawn.shape.index(max(drawn.shape))
    next_to = place[:widest] + [(place[widest] + 1) % drawn.shape[widest]] + place[widest + 1:]
    return drawn.at[tuple(place)].set(low).at[tuple(next_to)].set(high)


def levels(rng, dims, shards, low, high):
    gain, own = 1.0, jax.random.fold_in(rng, 6)
    for axis_at, parts in shards:
        steps = jnp.exp(jax.random.uniform(jax.random.fold_in(own, axis_at), (parts,), jnp.float32, low / len(shards), high / len(shards)))
        gain = gain * jnp.repeat(steps, dims[axis_at] // parts).reshape([-1 if axis == axis_at else 1 for axis in range(len(dims))])
    return gain


def deal_out(own_key, own, number, rows, count, top, limit, lean):
    order = jax.random.permutation(own_key, count)
    heavy_load, ordinary = portions_of(count, rows * top, limit, lean, True), portions_of(count, rows * top, limit, lean, False)
    places = jnp.arange(count)

    def named(sizes, offset_by):
        used = int((sizes > 0).sum())
        fixed = max(1, used // 4)
        moved = fixed + (places - fixed + offset_by * (used - fixed)) % max(1, count - fixed)
        return jnp.zeros((count,), jnp.int32).at[order[jnp.where(places < fixed, places, moved)]].set(jnp.asarray(sizes, jnp.int32))

    sizes = jnp.where(number % 4 == 0, named(heavy_load, number // 4), named(ordinary, number - number // 4 - 1))
    mixed = jax.random.permutation(jax.random.fold_in(own, 3), count)
    donor, receiver = mixed[0:count // 2 * 2:2], mixed[1:count // 2 * 2:2]
    margin = jnp.minimum(sizes[donor] - 1, limit - sizes[receiver]) // 2
    margin = jnp.where((donor == order[0]) | (receiver == order[0]) | (sizes[receiver] == 0), 0, jnp.maximum(margin, 0))
    moved = jax.random.randint(jax.random.fold_in(own, 4), (count // 2,), 0, 1 << 20) % (margin + 1)
    sizes = sizes.at[donor].add(-moved).at[receiver].add(moved)
    items = jnp.searchsorted(jnp.cumsum(sizes), jnp.arange(rows * top), side="right").astype(jnp.int32)
    table = items.reshape(top, rows).T
    table = table[jax.random.permutation(jax.random.fold_in(own, 1), rows)]
    offset_by = jax.random.randint(jax.random.fold_in(own, 2), (rows, 1), 0, top)
    return jnp.take_along_axis(table, (jnp.arange(top)[None, :] + offset_by) % top, axis=1)


def portions_of(number_of, total, reach, slope, full):
    weights = [(1 << 20) // math.isqrt(grade ** slope) + 1 for grade in range(1, number_of + 1)]
    largest = reach if full else min(reach, max(-(-total // number_of), total * weights[0] // sum(weights)))
    least = 1 if total - largest >= number_of - 1 else 0
    holding, rest = [largest] + [least] * (number_of - 1), total - largest - least * (number_of - 1)
    while rest > 0:
        movable = [i for i in range(1, number_of) if holding[i] < largest] or [i for i in range(1, number_of) if holding[i] < reach]
        pool, budget = sum([weights[i] for i in movable]), rest
        for i in movable:
            extra = min(reach - holding[i], max(1, budget * weights[i] // pool), rest)
            holding[i] = holding[i] + extra
            rest = rest - extra
    return np.array(holding)


def scatter_about(rng, shape, deviation, limit, split=(), held_as=jnp.bfloat16):
    values = jax.random.normal(rng, shape, jnp.float32) * deviation
    if len(split) > 0:
        values = levels(rng, shape, split, -0.22, 0.18) * values
    return jnp.clip(values, min=-limit, max=limit).astype(held_as)


def setup_inputs(seed: int = 0) -> dict:
    seeds = jax.random.split(jax.random.key(seed), 11)
    comps = scatter_about(seeds[0], (NX, NY, K), 1.0, 6.0, ((0, 128), (1, 4)))
    entry = place_ends(jax.random.randint(seeds[1], (NX, NY), 0, E_LOC), jax.random.fold_in(seeds[1], 1), 0, E_LOC - 1).astype(jnp.int32)
    dest_keys = jax.random.split(jax.random.fold_in(seeds[2], 1), N_WIDE * N_NARROW * (CX * CY) // (CX * CY))
    dest_turns = jax.random.permutation(jax.random.fold_in(seeds[2], 3), N_WIDE * N_NARROW * (CX * CY) // (CX * CY))
    dest = jax.vmap(lambda own, number: deal_out(jax.random.fold_in(seeds[2], 2), own, number, CX * CY, N_WIDE, 1, CAP, 0))(dest_keys, dest_turns).reshape((N_WIDE, N_NARROW, CX * CY, 1))
    slot_of_entry = jax.vmap(lambda own: jax.random.permutation(own, E_LOC))(jax.random.split(seeds[3], N_WIDE * N_NARROW)).reshape((N_WIDE, N_NARROW, E_LOC)).astype(jnp.int32)
    table_f0 = scatter_about(seeds[4], (N_WIDE, N_NARROW, E_LOC, K), 1.0, 6.0, ((0, 128), (1, 4)))
    table_x0 = scatter_about(seeds[5], (N_WIDE, N_NARROW, E_LOC, K), 1.0, 6.0, ((0, 128), (1, 4)))
    table_a = scatter_about(seeds[6], (N_WIDE, N_NARROW, E_LOC, K, K), K ** -0.5, 0.5, ((0, 128), (1, 4)))
    courant_x = jnp.clip(jax.random.uniform(seeds[7], (NX, NY), jnp.float32, -0.4, 0.4) * levels(seeds[7], (NX, NY), ((0, 128), (1, 4)), -0.4, 0.0), -0.4, 0.4)
    courant_y = jnp.clip(jax.random.uniform(seeds[8], (NX, NY), jnp.float32, -0.4, 0.4) * levels(seeds[8], (NX, NY), ((0, 128), (1, 4)), -0.4, 0.0), -0.4, 0.4)
    diffusion = jnp.clip(jnp.exp(jax.random.uniform(seeds[9], (K,), jnp.float32, math.log(0.02), math.log(0.1))), 0.02, 0.1)
    return {"comps": comps, "entry": entry, "dest": dest, "slot_of_entry": slot_of_entry, "table_f0": table_f0, "table_x0": table_x0, "table_a": table_a, "courant_x": courant_x, "courant_y": courant_y, "diffusion": diffusion}


def transport(padded, courant_x, courant_y, diffusion):
    center = padded[1:-1, 1:-1]
    east = padded[2:, 1:-1]
    west = padded[:-2, 1:-1]
    north = padded[1:-1, 2:]
    south = padded[1:-1, :-2]
    along_x = courant_x[:, :, None]
    along_y = courant_y[:, :, None]
    spread = diffusion[None, None, :]
    result = center - 0.5 * along_x * (east - west) + (0.5 * along_x * along_x + spread) * (east - 2.0 * center + west)
    return result - 0.5 * along_y * (north - south) + (0.5 * along_y * along_y + spread) * (north - 2.0 * center + south)


def reference(comps, entry, dest, slot_of_entry, table_f0, table_x0, table_a, courant_x, courant_y, diffusion):
    groups = N_WIDE * N_NARROW

    def blocks(field, trailing):
        shaped = field.reshape((N_WIDE, CX, N_NARROW, CY) + trailing)
        shaped = jnp.swapaxes(shaped, 1, 2)
        return shaped.reshape((groups, CX * CY) + trailing)

    states = blocks(comps, (K,))
    entries = blocks(entry, ())
    targets = dest.reshape(groups, CX * CY)

    def per_device(item):
        device_id, arrived, picks, owners = item
        narrow_id = device_id % N_NARROW
        slots = slot_of_entry[owners, narrow_id, picks]
        base_x = table_x0[owners, narrow_id, slots].astype(jnp.float32)
        base_f = table_f0[owners, narrow_id, slots].astype(jnp.float32)
        sens = table_a[owners, narrow_id, slots].astype(jnp.float32)
        offset = lax.optimization_barrier((arrived.astype(jnp.float32) - base_x).astype(jnp.bfloat16))
        moved = jnp.einsum("ck,ckj->cj", offset.astype(jnp.float32), sens)
        return (base_f + moved).astype(jnp.bfloat16)

    results = lax.map(per_device, (jnp.arange(groups, dtype=jnp.int32), states, entries, targets))
    field = jnp.swapaxes(results.reshape(N_WIDE, N_NARROW, CX, CY, K), 1, 2).reshape(NX, NY, K)
    padded = jnp.pad(field.astype(jnp.float32), ((1, 1), (1, 1), (0, 0)))
    return transport(padded, courant_x, courant_y, diffusion)
```

```python
import jax
import jax.numpy as jnp
from jax import lax
from jax.experimental import pallas as pl
from jax.experimental.pallas import tpu as pltpu
from jax.sharding import PartitionSpec as P

MESH = pl.DeviceIdType.MESH
F32 = jnp.float32
BF16 = jnp.bfloat16

SIDE = 8
SELF = 7
CAP = 12
SLAB = 32
SENT = 26
BACK = 24
ENTRY_ROW = 24
SLABS = 64
GROUP = 8 * SLAB
ENTRIES = 16


def far_first(i):
    odd = i % 2
    return (4 + odd * ((i + 1) // 2) + (1 - odd) * (8 - i // 2)) % SIDE


def rank_of_distance(d):
    t = lax.rem(d + 7, SIDE) - 3
    return jnp.where(t > 0, 2 * t - 1, -2 * t)


def iota(shape, dim):
    return lax.broadcasted_iota(jnp.int32, shape, dim)


def dot(a, b):
    return jnp.dot(a, b, preferred_element_type=F32)


def onehot(match):
    return jnp.where(match, 1.0, 0.0).astype(BF16)


def kernel(
    comps, entry, dest, slots, f0, x0, sens, cour_x, cour_y, diffusion, out,
    send, recv, res, ret, tab_a, tab_xf, col_p, acc, halo_src, halo_dst, edge_src, edge_dst,
    fwd_send, fwd_recv, ret_send, ret_recv, tab_send, tab_recv, halo_send, halo_recv,
):
    me = lax.axis_index("wide")
    mine_n = lax.axis_index("narrow")
    z, y, c = me // 16, (me // 2) % SIDE, me % 2

    def at(dz, dy):
        return {"wide": ((z + dz) % SIDE) * 16 + ((y + dy) % SIDE) * 2 + c}

    def ahead(a, b):
        return at(far_first((a + b) % SIDE), far_first(b))

    def behind(a, b):
        return at(SIDE - far_first((a + b) % SIDE), SIDE - far_first(b))

    def each_group(step):
        step(0, SIDE - 1)

        def body(a, carry):
            step(a, SIDE)
            return carry

        lax.fori_loop(1, SIDE, body, 0)

    partner = {"wide": me + 1 - 2 * c}
    above, below = {"wide": (me + 1) % 128}, {"wide": (me + 127) % 128}
    north, south = {"narrow": (mine_n + 1) % 4}, {"narrow": (mine_n + 3) % 4}

    recv[...] = jnp.zeros_like(recv)
    ret[...] = jnp.zeros_like(ret)
    tab_xf[pl.ds(32, 96), :] = jnp.zeros((96, 256), BF16)

    barrier = pltpu.get_barrier_semaphore()

    def greet(device):
        pl.semaphore_signal(barrier, inc=1, device_id=device, device_id_type=MESH)

    def greet_group(a, peers):
        for b in range(peers):
            greet(ahead(a, b))

    each_group(greet_group)
    for device in (partner, above, below, north, south):
        greet(device)

    pick = jnp.zeros((ENTRIES, 128), F32)
    for e in range(ENTRIES):
        s = slots[e]
        tab_a[c, pl.ds(e * 128, 128), :] = sens[s]
        pick = jnp.where((iota(pick.shape, 0) == e) & (iota(pick.shape, 1) == s), 1.0, pick)
    xf = jnp.concatenate([x0[...], f0[...]], axis=1)
    xf = jnp.concatenate([xf, jnp.zeros((112, 256), BF16)], axis=0)
    own_rows = pl.ds(pl.multiple_of(c * ENTRIES, ENTRIES), ENTRIES)
    tab_xf[own_rows, :] = dot(pick.astype(BF16), xf).astype(BF16)

    owner = dest[...]
    matches = [iota((128, 128), 0) == owner[i : i + 1, :] for i in range(8)]
    owned = jnp.concatenate([onehot(m) for m in matches], axis=0)
    before = onehot(iota((128, 128), 0) < iota((128, 128), 1))
    counts = dot(owned, jnp.concatenate([before, jnp.ones((128, 128), BF16)], axis=1))
    carry = jnp.zeros((128, 128), F32)
    ranks = []
    for i in range(8):
        part = counts[i * 128 : (i + 1) * 128]
        seen = jnp.where(matches[i], part[:, :128] + carry, 0.0)
        ranks.append(jnp.sum(seen, axis=0, keepdims=True))
        carry = carry + part[:, 128:]
    rank = jnp.concatenate(ranks, axis=0).astype(jnp.int32)

    to_core = owner % 2
    i_y = rank_of_distance((owner // 2 + SIDE - y) % SIDE)
    i_z = rank_of_distance((owner // 16 + SIDE - z) % SIDE)
    slab = ((i_z + SIDE - i_y) % SIDE) * SIDE + i_y
    row = to_core * CAP + rank
    place = slab * SLAB + row
    named = entry[...] + to_core * ENTRIES + 1

    place_t = jnp.transpose(place.astype(F32))
    row_t = jnp.transpose(row.astype(F32))
    named_t = jnp.transpose(named.astype(F32))
    lane = iota((128, 128), 1)
    lane_f = lane.astype(F32)
    names = []
    for i in range(8):
        col_p[pl.ds(i * 128, 128), :] = jnp.broadcast_to(place_t[:, i : i + 1], (128, 128))
        at_row = jnp.broadcast_to(row_t[:, i : i + 1], (128, 128)) == lane_f
        names.append(jnp.where(at_row, jnp.broadcast_to(named_t[:, i : i + 1], (128, 128)), 0.0))
    names = jnp.concatenate(names, axis=0).astype(BF16)
    in_slab = jnp.concatenate([onehot(iota((128, 128), 0) == slab[i : i + 1, :]) for i in range(8)], axis=1)
    entry_rows = dot(in_slab, names).astype(BF16)
    entry_place = jnp.where(lane[:1] < SLABS, lane[:1] * SLAB + ENTRY_ROW, -1)
    cells = jnp.concatenate([comps[...].reshape(1024, 128), entry_rows], axis=0)
    places = [place[i : i + 1, :] for i in range(8)] + [entry_place]

    def pack(a, carry):
        slot = iota((GROUP, 128), 0) + a * GROUP
        chosen = jnp.concatenate([onehot(slot == p) for p in places], axis=1)
        send[pl.ds(a * 8, 8)] = dot(chosen, cells).astype(BF16).reshape(8, SLAB, 128)
        return carry

    lax.fori_loop(0, SIDE, pack, 0)
    recv[SELF] = send[SELF]

    pl.semaphore_wait(barrier, SLABS - 1 + 5)

    def send_group(a, peers):
        for b in range(peers):
            pltpu.make_async_remote_copy(
                src_ref=send.at[a * 8 + b, pl.ds(0, SENT)],
                dst_ref=recv.at[a * 8 + b, pl.ds(0, SENT)],
                send_sem=fwd_send,
                recv_sem=fwd_recv.at[a],
                device_id=ahead(a, b),
                device_id_type=MESH,
            ).start()

    each_group(send_group)

    swaps = []
    for n, ref in enumerate((tab_a.at[c], tab_xf.at[own_rows])):
        swap = pltpu.make_async_remote_copy(
            src_ref=ref,
            dst_ref=ref,
            send_sem=tab_send.at[n],
            recv_sem=tab_recv.at[n],
            device_id=partner,
            device_id_type=MESH,
        )
        swap.start()
        swaps.append(swap)
    for swap in swaps:
        swap.wait()

    def wait_for(ref, sem):
        pltpu.make_async_copy(ref, ref, sem).wait()

    wide_lane = iota((GROUP, 128), 1)
    in_own_row = wide_lane == iota((GROUP, 128), 0) % SLAB
    spread = onehot(iota((GROUP, GROUP), 1) == (iota((GROUP, GROUP), 0) // SLAB) * SLAB + ENTRY_ROW)
    all_ones = jnp.ones((128, 128), BF16)

    def map_group(a, peers):
        wait_for(recv.at[pl.ds(a * 8, peers), pl.ds(0, SENT)], fwd_recv.at[a])
        states = recv[pl.ds(a * 8, 8)].reshape(GROUP, 128)
        named = jnp.where(in_own_row, dot(spread, states), 0.0).astype(BF16)
        named = dot(named, all_ones)
        base = dot(onehot(named == (wide_lane + 1).astype(F32)), tab_xf[...])
        offset = (states.astype(F32) - base[:, :128]).astype(BF16)
        chosen = [
            jnp.where(named == float(e + 1), offset.astype(F32), 0.0).astype(BF16) for e in range(2 * ENTRIES)
        ]
        moved = dot(jnp.concatenate(chosen, axis=1), tab_a[...].reshape(2 * ENTRIES * 128, 128))
        res[pl.ds(a * 8, 8)] = (base[:, 128:] + moved).astype(BF16).reshape(8, SLAB, 128)
        for b in range(peers):
            pltpu.make_async_remote_copy(
                src_ref=res.at[a * 8 + b, pl.ds(0, BACK)],
                dst_ref=ret.at[a * 8 + b, pl.ds(0, BACK)],
                send_sem=ret_send,
                recv_sem=ret_recv.at[a],
                device_id=behind(a, b),
                device_id_type=MESH,
            ).start()

    each_group(map_group)
    ret[SELF] = res[SELF]

    def placed(a, first, count):
        slot = (iota((count, 128), 1) + a * GROUP).astype(F32)
        at_col = col_p[pl.ds(first, count), :]
        chosen = jnp.concatenate([onehot(at_col == slot), onehot(at_col == slot + 128.0)], axis=1)
        return dot(chosen, ret[pl.ds(a * 8, 8)].reshape(GROUP, 128))

    acc[...] = jnp.zeros_like(acc)

    def place_group(a, peers):
        wait_for(ret.at[pl.ds(a * 8, peers), pl.ds(0, BACK)], ret_recv.at[a])
        acc[...] += placed(a, 0, 1024)

    each_group(place_group)

    halo_src[0] = acc[pl.ds(0, 128), :].astype(BF16)
    halo_src[1] = acc[pl.ds(896, 128), :].astype(BF16)
    field = [acc[pl.ds(i * 128, 128), :] for i in range(8)]
    edge_src[0] = jnp.concatenate([p[:1] for p in field], axis=0)
    edge_src[1] = jnp.concatenate([p[127:] for p in field], axis=0)
    halos = []
    for n, (src, dst, device) in enumerate(
        (
            (halo_src.at[0], halo_dst.at[1], below),
            (halo_src.at[1], halo_dst.at[0], above),
            (edge_src.at[0], edge_dst.at[1], south),
            (edge_src.at[1], edge_dst.at[0], north),
        )
    ):
        halo = pltpu.make_async_remote_copy(
            src_ref=src,
            dst_ref=dst,
            send_sem=halo_send.at[n],
            recv_sem=halo_recv.at[n],
            device_id=device,
            device_id_type=MESH,
        )
        halo.start()
        halos.append(halo)

    for halo in halos:
        halo.wait()

    spread_k = diffusion[...]
    cx_t = jnp.transpose(cour_x[...])
    cy_t = jnp.transpose(cour_y[...])
    low = jnp.where(me > 0, halo_dst[0].astype(F32), 0.0)
    high = jnp.where(me < 127, halo_dst[1].astype(F32), 0.0)
    edge_s = jnp.where(mine_n > 0, edge_dst[0], 0.0)
    edge_n = jnp.where(mine_n < 3, edge_dst[1], 0.0)
    for i in range(8):
        p = field[i]
        west = field[i - 1] if i > 0 else low
        east = field[i + 1] if i < 7 else high
        pn = jnp.concatenate([p[1:], edge_n[i : i + 1]], axis=0)
        ps = jnp.concatenate([edge_s[i : i + 1], p[:127]], axis=0)
        cx = jnp.broadcast_to(cx_t[:, i : i + 1], (128, 128))
        cy = jnp.broadcast_to(cy_t[:, i : i + 1], (128, 128))
        r = p - 0.5 * cx * (east - west) + (0.5 * cx * cx + spread_k) * (east - 2.0 * p + west)
        out[i] = r - 0.5 * cy * (pn - ps) + (0.5 * cy * cy + spread_k) * (pn - 2.0 * p + ps)

    for first, count in ((0, SELF), (SIDE, SLABS - SIDE)):
        wait_for(send.at[pl.ds(first, count), pl.ds(0, SENT)], fwd_send)
        wait_for(res.at[pl.ds(first, count), pl.ds(0, BACK)], ret_send)


def body(comps, entry, dest, slot_of_entry, table_f0, table_x0, table_a, courant_x, courant_y, diffusion):
    vmem = pl.BlockSpec(memory_space=pltpu.VMEM)
    smem = pl.BlockSpec(memory_space=pltpu.SMEM)
    dma = pltpu.SemaphoreType.DMA
    return pl.pallas_call(
        kernel,
        out_shape=jax.ShapeDtypeStruct(comps.shape, F32),
        in_specs=[vmem, vmem, vmem, smem] + [vmem] * 6,
        out_specs=vmem,
        scratch_shapes=[
            pltpu.VMEM((SLABS, SLAB, 128), BF16),
            pltpu.VMEM((SLABS, SLAB, 128), BF16),
            pltpu.VMEM((SLABS, SLAB, 128), BF16),
            pltpu.VMEM((SLABS, SLAB, 128), BF16),
            pltpu.VMEM((2, ENTRIES * 128, 128), BF16),
            pltpu.VMEM((128, 256), BF16),
            pltpu.VMEM((1024, 128), F32),
            pltpu.VMEM((1024, 128), F32),
            pltpu.VMEM((2, 128, 128), BF16),
            pltpu.VMEM((2, 128, 128), BF16),
            pltpu.VMEM((2, 8, 128), F32),
            pltpu.VMEM((2, 8, 128), F32),
            dma(()),
            dma((SIDE,)),
            dma(()),
            dma((SIDE,)),
            dma((2,)),
            dma((2,)),
            dma((4,)),
            dma((4,)),
        ],
        compiler_params=pltpu.CompilerParams(
            collective_id=0, has_side_effects=True, vmem_limit_bytes=48 * 1024 * 1024
        ),
        name="chemistry",
    )(
        comps,
        entry,
        dest.reshape(entry.shape),
        slot_of_entry.reshape(ENTRIES),
        table_f0[0, 0],
        table_x0[0, 0],
        table_a[0, 0],
        courant_x,
        courant_y,
        diffusion.reshape(1, -1),
    )


def solution(mesh):
    in_specs = (
        P("wide", "narrow", None),
        P("wide", "narrow"),
        P("wide", "narrow", None, None),
        P("wide", "narrow", None),
        P("wide", "narrow", None, None),
        P("wide", "narrow", None, None),
        P("wide", "narrow", None, None, None),
        P("wide", "narrow"),
        P("wide", "narrow"),
        P(),
    )
    out_specs = P("wide", "narrow", None)
    return jax.shard_map(body, mesh=mesh, in_specs=in_specs, out_specs=out_specs, check_vma=False)
```

```python
import jax
import jax.numpy as jnp
from jax import lax
from jax.experimental import pallas as pl
from jax.experimental.pallas import tpu as pltpu
from jax.sharding import PartitionSpec as P

MESH = pl.DeviceIdType.MESH
F32 = jnp.float32
BF16 = jnp.bfloat16

SIDE = 8
SELF = 55
SELF_GROUP = SELF // SIDE
CAP = 12
SLAB = 32
SENT = 26
BACK = 24
ENTRY_ROW = 24
SLABS = 64
GROUP = 8 * SLAB
ENTRIES = 16


def far_first(i):
    odd = i % 2
    return (4 + odd * ((i + 1) // 2) + (1 - odd) * (8 - i // 2)) % SIDE


def rank_of_distance(d):
    t = lax.rem(d + 7, SIDE) - 3
    return jnp.where(t > 0, 2 * t - 1, -2 * t)


def iota(shape, dim):
    return lax.broadcasted_iota(jnp.int32, shape, dim)


def dot(a, b):
    return jnp.dot(a, b, preferred_element_type=F32)


def onehot(match):
    return jnp.where(match, 1.0, 0.0).astype(BF16)


def across(column):
    return jnp.broadcast_to(column, (column.shape[0], 128))


def kernel(
    comps_in, entry_in, dest_in, slots_in, f0_in, x0_in, sens_in, cour_x_in, cour_y_in, diffusion_in, out,
    comps, entry, dest, slots, f0, x0, sens, cour_x, cour_y, diffusion, in_sem,
    send, recv, res, ret, tab_a, tab_xf, col_p, acc, halo_src, halo_dst, edge_src, edge_dst,
    fwd_send, fwd_recv, ret_send, ret_recv, tab_send, tab_recv, halo_send, halo_recv,
):
    me = lax.axis_index("wide")
    mine_n = lax.axis_index("narrow")
    z, y, c = me // 16, (me // 2) % SIDE, me % 2

    def at(dz, dy):
        return {"wide": ((z + dz) % SIDE) * 16 + ((y + dy) % SIDE) * 2 + c}

    def ahead(a, b):
        return at(far_first((a + SIDE - b) % SIDE), far_first(b))

    def behind(a, b):
        return at(SIDE - far_first((a + SIDE - b) % SIDE), SIDE - far_first(b))

    def each_group(step, last=SIDE):
        def body(a, carry):
            step(a, SIDE)
            return carry

        lax.fori_loop(0, SELF_GROUP, body, 0)
        step(SELF_GROUP, SIDE - 1)
        for a in range(SELF_GROUP + 1, last):
            step(a, SIDE)

    def remote(src, dst, send_sem, recv_sem, device):
        copy = pltpu.make_async_remote_copy(
            src_ref=src,
            dst_ref=dst,
            send_sem=send_sem,
            recv_sem=recv_sem,
            device_id=device,
            device_id_type=MESH,
        )
        copy.start()
        return copy

    def wait_for(ref, sem):
        pltpu.make_async_copy(ref, ref, sem).wait()

    partner = {"wide": me + 1 - 2 * c}
    above, below = {"wide": (me + 1) % 128}, {"wide": (me + 127) % 128}
    north, south = {"narrow": (mine_n + 1) % 4}, {"narrow": (mine_n + 3) % 4}

    loads = [
        pltpu.make_async_copy(src, dst, in_sem.at[n])
        for n, (src, dst) in enumerate(
            (
                (dest_in, dest),
                (entry_in, entry),
                (comps_in, comps),
                (slots_in, slots),
                (f0_in, f0),
                (x0_in, x0),
                (sens_in, sens),
                (cour_x_in, cour_x),
                (cour_y_in, cour_y),
                (diffusion_in, diffusion),
            )
        )
    ]
    for load in loads:
        load.start()

    recv[...] = jnp.zeros_like(recv)
    ret[...] = jnp.zeros_like(ret)
    tab_xf[pl.ds(32, 96), :] = jnp.zeros((96, 256), BF16)

    barrier = pltpu.get_barrier_semaphore()

    def greet(device):
        pl.semaphore_signal(barrier, inc=1, device_id=device, device_id_type=MESH)

    def greet_some(u, carry):
        for b in range(SIDE):
            greet(at(far_first(2 * (u % 4) + b // 4), far_first(4 * (u // 4) + b % 4)))
        return carry

    lax.fori_loop(0, SIDE - 1, greet_some, 0)
    for b in range(SIDE - 1):
        greet(at(far_first(6 + b // 4), far_first(4 + b % 4)))
    for device in (above, below, north, south, partner):
        greet(device)

    for load in loads:
        load.wait()

    owner = dest[...]
    matches = [iota((128, 128), 0) == owner[i : i + 1, :] for i in range(8)]
    owned = jnp.concatenate([onehot(m) for m in matches], axis=0)
    before = onehot(iota((128, 128), 0) < iota((128, 128), 1))
    counts = dot(owned, jnp.concatenate([before, jnp.ones((128, 128), BF16)], axis=1))
    carry = jnp.zeros((128, 128), F32)
    ranks = []
    for i in range(8):
        part = counts[i * 128 : (i + 1) * 128]
        seen = jnp.where(matches[i], part[:, :128] + carry, 0.0)
        ranks.append(jnp.sum(seen, axis=0, keepdims=True))
        carry = carry + part[:, 128:]
    rank = jnp.concatenate(ranks, axis=0).astype(jnp.int32)

    to_core = owner % 2
    i_y = rank_of_distance((owner // 2 + SIDE - y) % SIDE)
    i_z = rank_of_distance((owner // 16 + SIDE - z) % SIDE)
    slab = ((i_z + i_y) % SIDE) * SIDE + i_y
    row = to_core * CAP + rank
    place = slab * SLAB + row
    named = entry[...] + to_core * ENTRIES + 1

    place_t = jnp.transpose(place.astype(F32))
    row_t = jnp.transpose(row.astype(F32))
    named_t = jnp.transpose(named.astype(F32))
    lane = iota((128, 128), 1)
    lane_f = lane.astype(F32)
    names = []
    for i in range(8):
        col_p[pl.ds(i * 128, 128), :] = across(place_t[:, i : i + 1])
        names.append(jnp.where(across(row_t[:, i : i + 1]) == lane_f, across(named_t[:, i : i + 1]), 0.0))
    names = jnp.concatenate(names, axis=0).astype(BF16)
    in_slab = jnp.concatenate([onehot(iota((128, 128), 0) == slab[i : i + 1, :]) for i in range(8)], axis=1)
    entry_rows = dot(in_slab, names).astype(BF16)
    entry_place = jnp.where(lane[:1] < SLABS, lane[:1] * SLAB + ENTRY_ROW, -1)
    cells = jnp.concatenate([comps[...].reshape(1024, 128), entry_rows], axis=0)
    places = [place[i : i + 1, :] for i in range(8)] + [entry_place]

    pick = jnp.zeros((ENTRIES, 128), F32)
    for e in range(ENTRIES):
        s = slots[e]
        tab_a[c, pl.ds(e * 128, 128), :] = sens[s]
        pick = jnp.where((iota(pick.shape, 0) == e) & (iota(pick.shape, 1) == s), 1.0, pick)
    xf = jnp.concatenate([x0[...], f0[...]], axis=1)
    xf = jnp.concatenate([xf, jnp.zeros((112, 256), BF16)], axis=0)
    own_rows = pl.ds(pl.multiple_of(c * ENTRIES, ENTRIES), ENTRIES)
    tab_xf[own_rows, :] = dot(pick.astype(BF16), xf).astype(BF16)

    pl.semaphore_wait(barrier, SLABS - 1 + 5)

    swaps = [
        remote(ref, ref, tab_send.at[n], tab_recv.at[n], partner)
        for n, ref in enumerate((tab_a.at[c], tab_xf.at[own_rows]))
    ]

    def send_group(a, peers):
        slot = iota((GROUP, 128), 0) + a * GROUP
        chosen = jnp.concatenate([onehot(slot == p) for p in places], axis=1)
        send[pl.ds(a * 8, 8)] = dot(chosen, cells).astype(BF16).reshape(8, SLAB, 128)
        for b in range(peers):
            k = a * 8 + b
            sent = pl.ds(0, SENT)
            remote(send.at[k, sent], recv.at[k, sent], fwd_send, fwd_recv.at[a], ahead(a, b))

    each_group(send_group)
    recv[SELF] = send[SELF]
    for swap in swaps:
        swap.wait()

    wide_lane = iota((GROUP, 128), 1)
    in_own_row = wide_lane == iota((GROUP, 128), 0) % SLAB
    spread = onehot(iota((GROUP, GROUP), 1) == (iota((GROUP, GROUP), 0) // SLAB) * SLAB + ENTRY_ROW)
    all_ones = jnp.ones((128, 128), BF16)

    def map_group(a, peers):
        wait_for(recv.at[pl.ds(a * 8, peers), pl.ds(0, SENT)], fwd_recv.at[a])
        states = recv[pl.ds(a * 8, 8)].reshape(GROUP, 128)
        named = jnp.where(in_own_row, dot(spread, states), 0.0).astype(BF16)
        named = dot(named, all_ones)
        base = dot(onehot(named == (wide_lane + 1).astype(F32)), tab_xf[...])
        offset = (states.astype(F32) - base[:, :128]).astype(BF16)
        chosen = [
            jnp.where(named == float(e + 1), offset.astype(F32), 0.0).astype(BF16) for e in range(2 * ENTRIES)
        ]
        moved = dot(jnp.concatenate(chosen, axis=1), tab_a[...].reshape(2 * ENTRIES * 128, 128))
        res[pl.ds(a * 8, 8)] = (base[:, 128:] + moved).astype(BF16).reshape(8, SLAB, 128)
        for b in range(peers):
            k = a * 8 + b
            back = pl.ds(0, BACK)
            remote(res.at[k, back], ret.at[k, back], ret_send, ret_recv.at[a], behind(a, b))

    each_group(map_group)
    ret[SELF] = res[SELF]

    def placed(a, first, count):
        slot = (iota((count, 128), 1) + a * GROUP).astype(F32)
        at_col = col_p[pl.ds(first, count), :]
        chosen = jnp.concatenate([onehot(at_col == slot), onehot(at_col == slot + 128.0)], axis=1)
        return dot(chosen, ret[pl.ds(a * 8, 8)].reshape(GROUP, 128))

    acc[...] = jnp.zeros_like(acc)

    def place_group(a, peers):
        wait_for(ret.at[pl.ds(a * 8, peers), pl.ds(0, BACK)], ret_recv.at[a])
        acc[...] += placed(a, 0, 1024)

    last = SIDE - 1
    each_group(place_group, last)
    wait_for(ret.at[pl.ds(last * 8, 8), pl.ds(0, BACK)], ret_recv.at[last])

    def finish(first, count):
        done = acc[pl.ds(first, count), :] + placed(last, first, count)
        acc[pl.ds(first, count), :] = done
        return done

    def halo(n, src, dst, device):
        return remote(src, dst, halo_send.at[n], halo_recv.at[n], device)

    halo_src[0] = finish(0, 128).astype(BF16)
    halos = [halo(0, halo_src.at[0], halo_dst.at[1], below)]
    halo_src[1] = finish(896, 128).astype(BF16)
    halos.append(halo(1, halo_src.at[1], halo_dst.at[0], above))
    finish(128, 768)
    field = [acc[pl.ds(i * 128, 128), :] for i in range(8)]
    edge_src[0] = jnp.concatenate([p[:1] for p in field], axis=0)
    edge_src[1] = jnp.concatenate([p[127:] for p in field], axis=0)
    halos.append(halo(2, edge_src.at[0], edge_dst.at[1], south))
    halos.append(halo(3, edge_src.at[1], edge_dst.at[0], north))

    species = diffusion[...]
    cx_t = jnp.transpose(cour_x[...])
    cy_t = jnp.transpose(cour_y[...])
    nothing = jnp.zeros((128, 128), F32)
    no_row = jnp.zeros((1, 128), F32)
    for i in range(8):
        p = field[i]
        west = field[i - 1] if i > 0 else nothing
        east = field[i + 1] if i < 7 else nothing
        pn = jnp.concatenate([p[1:], no_row], axis=0)
        ps = jnp.concatenate([no_row, p[:127]], axis=0)
        cx, cy = across(cx_t[:, i : i + 1]), across(cy_t[:, i : i + 1])
        r = p - 0.5 * cx * (east - west) + (0.5 * cx * cx + species) * (east - 2.0 * p + west)
        out[i] = r - 0.5 * cy * (pn - ps) + (0.5 * cy * cy + species) * (pn - 2.0 * p + ps)

    for copy in halos:
        copy.wait()

    def weight(courant, sign):
        return sign * 0.5 * courant + 0.5 * courant * courant + species

    low = jnp.where(me > 0, halo_dst[0].astype(F32), 0.0)
    high = jnp.where(me < 127, halo_dst[1].astype(F32), 0.0)
    edge_s = jnp.where(mine_n > 0, edge_dst[0], 0.0)
    edge_n = jnp.where(mine_n < 3, edge_dst[1], 0.0)
    out[0] += low * weight(across(cx_t[:, 0:1]), 1.0)
    out[7] += high * weight(across(cx_t[:, 7:8]), -1.0)
    edge_s = edge_s * weight(across(cour_y[:, 0:1]), 1.0)
    edge_n = edge_n * weight(across(cour_y[:, 127:128]), -1.0)
    for i in range(8):
        out[i, 0:1, :] += edge_s[i : i + 1]
        out[i, 127:128, :] += edge_n[i : i + 1]

    for first, count in ((0, SELF), (SELF + 1, SLABS - SELF - 1)):
        wait_for(send.at[pl.ds(first, count), pl.ds(0, SENT)], fwd_send)
        wait_for(res.at[pl.ds(first, count), pl.ds(0, BACK)], ret_send)


def body(comps, entry, dest, slot_of_entry, table_f0, table_x0, table_a, courant_x, courant_y, diffusion):
    args = (
        comps,
        entry,
        dest.reshape(entry.shape),
        slot_of_entry.reshape(ENTRIES),
        table_f0[0, 0],
        table_x0[0, 0],
        table_a[0, 0],
        courant_x,
        courant_y,
        diffusion.reshape(1, -1),
    )
    hbm = pl.BlockSpec(memory_space=pltpu.HBM)
    dma = pltpu.SemaphoreType.DMA
    return pl.pallas_call(
        kernel,
        out_shape=jax.ShapeDtypeStruct(comps.shape, F32),
        in_specs=[hbm] * len(args),
        out_specs=pl.BlockSpec(memory_space=pltpu.VMEM),
        scratch_shapes=[
            pltpu.SMEM(a.shape, a.dtype) if n == 3 else pltpu.VMEM(a.shape, a.dtype) for n, a in enumerate(args)
        ]
        + [
            dma((len(args),)),
            pltpu.VMEM((SLABS, SLAB, 128), BF16),
            pltpu.VMEM((SLABS, SLAB, 128), BF16),
            pltpu.VMEM((SLABS, SLAB, 128), BF16),
            pltpu.VMEM((SLABS, SLAB, 128), BF16),
            pltpu.VMEM((2, ENTRIES * 128, 128), BF16),
            pltpu.VMEM((128, 256), BF16),
            pltpu.VMEM((1024, 128), F32),
            pltpu.VMEM((1024, 128), F32),
            pltpu.VMEM((2, 128, 128), BF16),
            pltpu.VMEM((2, 128, 128), BF16),
            pltpu.VMEM((2, 8, 128), F32),
            pltpu.VMEM((2, 8, 128), F32),
            dma(()),
            dma((SIDE,)),
            dma(()),
            dma((SIDE,)),
            dma((2,)),
            dma((2,)),
            dma((4,)),
            dma((4,)),
        ],
        compiler_params=pltpu.CompilerParams(
            collective_id=0, has_side_effects=True, vmem_limit_bytes=32 * 1024 * 1024
        ),
        name="chemistry",
    )(*[pltpu.with_memory_space_constraint(a, pltpu.HBM) for a in args])


def solution(mesh):
    in_specs = (
        P("wide", "narrow", None),
        P("wide", "narrow"),
        P("wide", "narrow", None, None),
        P("wide", "narrow", None),
        P("wide", "narrow", None, None),
        P("wide", "narrow", None, None),
        P("wide", "narrow", None, None, None),
        P("wide", "narrow"),
        P("wide", "narrow"),
        P(),
    )
    out_specs = P("wide", "narrow", None)
    return jax.shard_map(body, mesh=mesh, in_specs=in_specs, out_specs=out_specs, check_vma=False)
```

```python
import jax
import jax.numpy as jnp
from jax import lax
from jax.experimental import pallas as pl
from jax.experimental.pallas import tpu as pltpu
from jax.sharding import PartitionSpec as P

MESH = pl.DeviceIdType.MESH
F32 = jnp.float32
BF16 = jnp.bfloat16

SIDE = 8


def hops(offset):
    return [min(d, SIDE - d) for d in offset]


def longest_first(offset):
    far, (dz, dy) = hops(offset), offset
    return (-sum(far), -max(far), far[0] > far[1], (dz > SIDE // 2) != (dy > SIDE // 2), dz, dy)


OTHERS = sorted([(dz, dy) for dz in range(SIDE) for dy in range(SIDE) if (dz, dy) != (0, 0)], key=longest_first)
NEAR = [o for o in OTHERS if sum(hops(o)) <= 3]
OFFSETS = NEAR + [o for o in OTHERS if o not in NEAR] + [(0, 0)]
NEAR_GROUPS = len(NEAR) // SIDE
COLUMN = [o for o in OTHERS if o[1] == 0]
FIRST = [o for o in OTHERS if o in NEAR or 0 in o]
SELF = len(OFFSETS) - 1
CAP = 12
SLAB = 32
SENT = 26
BACK = 24
ENTRY_ROW = 24
SLABS = 64
GROUP = 8 * SLAB
ENTRIES = 16


def iota(shape, dim):
    return lax.broadcasted_iota(jnp.int32, shape, dim)


def dot(a, b):
    return jnp.dot(a, b, preferred_element_type=F32)


def onehot(match):
    return jnp.where(match, 1.0, 0.0).astype(BF16)


def across(column):
    return jnp.broadcast_to(column, (column.shape[0], 128))


def kernel(
    comps_in, entry_in, dest_in, slots_in, f0_in, x0_in, sens_in, cour_x_in, cour_y_in, diffusion_in, out,
    comps, entry, dest, slots, f0, x0, sens, cour_x, cour_y, diffusion, in_sem,
    send, recv, res, ret, tab_a, tab_xf, col_p, acc, halo_src, halo_dst, edge_src, edge_dst,
    fwd_send, fwd_recv, ret_send, ret_recv, tab_send, tab_recv, halo_send, halo_recv, row_in,
):
    me = lax.axis_index("wide")
    mine_n = lax.axis_index("narrow")
    z, y, c = me // 16, (me // 2) % SIDE, me % 2

    rows_z = [(z + d) % SIDE * 16 for d in range(SIDE)]
    rows_y = [(y + d) % SIDE * 2 + c for d in range(SIDE)]

    def at(dz, dy):
        return {"wide": rows_z[dz % SIDE] + rows_y[dy % SIDE]}

    def behind(a, b):
        dz, dy = OFFSETS[b]
        for g in range(1, SIDE):
            dz = jnp.where(a == g, OFFSETS[g * 8 + b][0], dz)
            dy = jnp.where(a == g, OFFSETS[g * 8 + b][1], dy)
        return {"wide": (z + SIDE - dz) % SIDE * 16 + (y + SIDE - dy) % SIDE * 2 + c}

    def each_group(step, last=SIDE):
        def body(a, carry):
            step(a, SIDE)
            return carry

        lax.fori_loop(0, SIDE - 1, body, 0)
        if last == SIDE:
            step(SIDE - 1, SIDE - 1)

    def remote(src, dst, send_sem, recv_sem, device):
        copy = pltpu.make_async_remote_copy(
            src_ref=src,
            dst_ref=dst,
            send_sem=send_sem,
            recv_sem=recv_sem,
            device_id=device,
            device_id_type=MESH,
        )
        copy.start()
        return copy

    def wait_for(ref, sem):
        pltpu.make_async_copy(ref, ref, sem).wait()

    partner = {"wide": me + 1 - 2 * c}
    above, below = {"wide": (me + 1) % 128}, {"wide": (me + 127) % 128}
    north, south = {"narrow": (mine_n + 1) % 4}, {"narrow": (mine_n + 3) % 4}

    loads = [
        pltpu.make_async_copy(src, dst, in_sem.at[n])
        for n, (src, dst) in enumerate(
            (
                (dest_in, dest),
                (entry_in, entry),
                (comps_in, comps),
                (slots_in, slots),
                (f0_in, f0),
                (x0_in, x0),
                (sens_in, sens),
                (cour_x_in, cour_x),
                (cour_y_in, cour_y),
                (diffusion_in, diffusion),
            )
        )
    ]
    for load in loads:
        load.start()

    recv[...] = jnp.zeros_like(recv)

    barrier = pltpu.get_barrier_semaphore()

    def greet(device):
        pl.semaphore_signal(barrier, inc=1, device_id=device, device_id_type=MESH)

    for offset in FIRST:
        greet(at(*offset))
    for device in (above, below, north, south, partner):
        greet(device)

    ret[...] = jnp.zeros_like(ret)
    tab_xf[pl.ds(32, 96), :] = jnp.zeros((96, 256), BF16)
    for load in loads[:3]:
        load.wait()

    owner = dest[...]
    matches = [iota((128, 128), 0) == owner[i : i + 1, :] for i in range(8)]
    owned = jnp.concatenate([onehot(m) for m in matches], axis=0)
    before = onehot(iota((128, 128), 0) < iota((128, 128), 1))
    counts = dot(owned, jnp.concatenate([before, jnp.ones((128, 128), BF16)], axis=1))
    carry = jnp.zeros((128, 128), F32)
    ranks = []
    for i in range(8):
        part = counts[i * 128 : (i + 1) * 128]
        seen = jnp.where(matches[i], part[:, :128] + carry, 0.0)
        ranks.append(jnp.sum(seen, axis=0, keepdims=True))
        carry = carry + part[:, 128:]
    rank = jnp.concatenate(ranks, axis=0).astype(jnp.int32)

    to_core = owner % 2
    offset = (owner // 16 + SIDE - z) % SIDE * SIDE + (owner // 2 + SIDE - y) % SIDE
    slab = jnp.zeros_like(owner)
    for k, (dz, dy) in enumerate(OFFSETS):
        slab = jnp.where(offset == dz * SIDE + dy, k, slab)
    row = to_core * CAP + rank
    place = slab * SLAB + row
    named = entry[...] + to_core * ENTRIES + 1

    place_t = jnp.transpose(place.astype(F32))
    row_t = jnp.transpose(row.astype(F32))
    named_t = jnp.transpose(named.astype(F32))
    lane = iota((128, 128), 1)
    lane_f = lane.astype(F32)
    names = []
    for i in range(8):
        col_p[pl.ds(i * 128, 128), :] = across(place_t[:, i : i + 1])
        names.append(jnp.where(across(row_t[:, i : i + 1]) == lane_f, across(named_t[:, i : i + 1]), 0.0))
    names = jnp.concatenate(names, axis=0).astype(BF16)
    in_slab = jnp.concatenate([onehot(iota((128, 128), 0) == slab[i : i + 1, :]) for i in range(8)], axis=1)
    entry_rows = dot(in_slab, names).astype(BF16)
    entry_place = jnp.where(lane[:1] < SLABS, lane[:1] * SLAB + ENTRY_ROW, -1)
    cells = jnp.concatenate([comps[...].reshape(1024, 128), entry_rows], axis=0)
    places = [place[i : i + 1, :] for i in range(8)] + [entry_place]

    def pack(a, carry):
        slot = iota((GROUP, 128), 0) + a * GROUP
        chosen = jnp.concatenate([onehot(slot == p) for p in places], axis=1)
        send[pl.ds(a * 8, 8)] = dot(chosen, cells).astype(BF16).reshape(8, SLAB, 128)
        return carry

    lax.fori_loop(0, NEAR_GROUPS, pack, 0)

    pl.semaphore_wait(barrier, len(FIRST) + 5)

    for offset in COLUMN:
        pl.semaphore_signal(row_in, inc=1, device_id=at(*offset), device_id_type=MESH)

    def send_groups(first, last):
        sent = pl.ds(0, SENT)
        for k in range(first * 8, min(last * 8, SELF)):
            remote(send.at[k, sent], recv.at[k, sent], fwd_send, fwd_recv.at[k // 8], at(*OFFSETS[k]))

    send_groups(0, NEAR_GROUPS)

    for load in loads[3:]:
        load.wait()

    pick = jnp.zeros((ENTRIES, 128), F32)
    for e in range(ENTRIES):
        s = slots[e]
        tab_a[c, pl.ds(e * 128, 128), :] = sens[s]
        pick = jnp.where((iota(pick.shape, 0) == e) & (iota(pick.shape, 1) == s), 1.0, pick)
    xf = jnp.concatenate([x0[...], f0[...]], axis=1)
    xf = jnp.concatenate([xf, jnp.zeros((112, 256), BF16)], axis=0)
    own_rows = pl.ds(pl.multiple_of(c * ENTRIES, ENTRIES), ENTRIES)
    tab_xf[own_rows, :] = dot(pick.astype(BF16), xf).astype(BF16)

    swaps = [
        remote(ref, ref, tab_send.at[n], tab_recv.at[n], partner)
        for n, ref in enumerate((tab_a.at[c], tab_xf.at[own_rows]))
    ]

    lax.fori_loop(NEAR_GROUPS, SIDE, pack, 0)
    recv[SELF] = send[SELF]
    pl.semaphore_wait(row_in, len(COLUMN))
    send_groups(NEAR_GROUPS, SIDE)
    for swap in swaps:
        swap.wait()

    wide_lane = iota((GROUP, 128), 1)
    in_own_row = wide_lane == iota((GROUP, 128), 0) % SLAB
    spread = onehot(iota((GROUP, GROUP), 1) == (iota((GROUP, GROUP), 0) // SLAB) * SLAB + ENTRY_ROW)
    all_ones = jnp.ones((128, 128), BF16)

    def map_group(a, peers):
        wait_for(recv.at[pl.ds(a * 8, peers), pl.ds(0, SENT)], fwd_recv.at[a])
        states = recv[pl.ds(a * 8, 8)].reshape(GROUP, 128)
        named = jnp.where(in_own_row, dot(spread, states), 0.0).astype(BF16)
        named = dot(named, all_ones)
        base = dot(onehot(named == (wide_lane + 1).astype(F32)), tab_xf[...])
        offset = (states.astype(F32) - base[:, :128]).astype(BF16)
        names = named.astype(BF16)
        chosen = [jnp.where(names == jnp.bfloat16(e + 1), offset, jnp.bfloat16(0)) for e in range(2 * ENTRIES)]
        moved = dot(jnp.concatenate(chosen, axis=1), tab_a[...].reshape(2 * ENTRIES * 128, 128))
        res[pl.ds(a * 8, 8)] = (base[:, 128:] + moved).astype(BF16).reshape(8, SLAB, 128)
        for b in range(peers):
            k = a * 8 + b
            back = pl.ds(0, BACK)
            remote(res.at[k, back], ret.at[k, back], ret_send, ret_recv.at[a], behind(a, b))

    each_group(map_group)
    ret[SELF] = res[SELF]

    def placed(a, first, count):
        slot = (iota((count, 128), 1) + a * GROUP).astype(F32)
        at_col = col_p[pl.ds(first, count), :]
        chosen = jnp.concatenate([onehot(at_col == slot), onehot(at_col == slot + 128.0)], axis=1)
        return dot(chosen, ret[pl.ds(a * 8, 8)].reshape(GROUP, 128))

    acc[...] = jnp.zeros_like(acc)

    def place_group(a, peers):
        wait_for(ret.at[pl.ds(a * 8, peers), pl.ds(0, BACK)], ret_recv.at[a])
        acc[...] += placed(a, 0, 1024)

    last = SIDE - 1
    each_group(place_group, last)
    wait_for(ret.at[pl.ds(last * 8, 7), pl.ds(0, BACK)], ret_recv.at[last])

    def finish(first, count):
        done = acc[pl.ds(first, count), :] + placed(last, first, count)
        acc[pl.ds(first, count), :] = done
        return done

    def halo(n, src, dst, device):
        return remote(src, dst, halo_send.at[n], halo_recv.at[n], device)

    halo_src[0] = finish(0, 128).astype(BF16)
    halos = [halo(0, halo_src.at[0], halo_dst.at[1], below)]
    halo_src[1] = finish(896, 128).astype(BF16)
    halos.append(halo(1, halo_src.at[1], halo_dst.at[0], above))
    finish(128, 768)
    field = [acc[pl.ds(i * 128, 128), :] for i in range(8)]
    edge_src[0] = jnp.concatenate([p[:1] for p in field], axis=0)
    edge_src[1] = jnp.concatenate([p[127:] for p in field], axis=0)
    halos.append(halo(2, edge_src.at[0], edge_dst.at[1], south))
    halos.append(halo(3, edge_src.at[1], edge_dst.at[0], north))

    species = diffusion[...]
    cx_t = jnp.transpose(cour_x[...])
    cy_t = jnp.transpose(cour_y[...])
    nothing = jnp.zeros((128, 128), F32)
    no_row = jnp.zeros((1, 128), F32)
    for i in range(8):
        p = field[i]
        west = field[i - 1] if i > 0 else nothing
        east = field[i + 1] if i < 7 else nothing
        pn = jnp.concatenate([p[1:], no_row], axis=0)
        ps = jnp.concatenate([no_row, p[:127]], axis=0)
        cx, cy = across(cx_t[:, i : i + 1]), across(cy_t[:, i : i + 1])
        r = p - 0.5 * cx * (east - west) + (0.5 * cx * cx + species) * (east - 2.0 * p + west)
        out[i] = r - 0.5 * cy * (pn - ps) + (0.5 * cy * cy + species) * (pn - 2.0 * p + ps)

    for copy in halos:
        copy.wait()

    def weight(courant, sign):
        return sign * 0.5 * courant + 0.5 * courant * courant + species

    low = jnp.where(me > 0, halo_dst[0].astype(F32), 0.0)
    high = jnp.where(me < 127, halo_dst[1].astype(F32), 0.0)
    edge_s = jnp.where(mine_n > 0, edge_dst[0], 0.0)
    edge_n = jnp.where(mine_n < 3, edge_dst[1], 0.0)
    out[0] += low * weight(across(cx_t[:, 0:1]), 1.0)
    out[7] += high * weight(across(cx_t[:, 7:8]), -1.0)
    edge_s = edge_s * weight(across(cour_y[:, 0:1]), 1.0)
    edge_n = edge_n * weight(across(cour_y[:, 127:128]), -1.0)
    for i in range(8):
        out[i, 0:1, :] += edge_s[i : i + 1]
        out[i, 127:128, :] += edge_n[i : i + 1]

    wait_for(send.at[pl.ds(0, SELF), pl.ds(0, SENT)], fwd_send)
    wait_for(res.at[pl.ds(0, SELF), pl.ds(0, BACK)], ret_send)


def body(comps, entry, dest, slot_of_entry, table_f0, table_x0, table_a, courant_x, courant_y, diffusion):
    args = (
        comps,
        entry,
        dest.reshape(entry.shape),
        slot_of_entry.reshape(ENTRIES),
        table_f0[0, 0],
        table_x0[0, 0],
        table_a[0, 0],
        courant_x,
        courant_y,
        diffusion.reshape(1, -1),
    )
    hbm = pl.BlockSpec(memory_space=pltpu.HBM)
    dma = pltpu.SemaphoreType.DMA
    return pl.pallas_call(
        kernel,
        out_shape=jax.ShapeDtypeStruct(comps.shape, F32),
        in_specs=[hbm] * len(args),
        out_specs=pl.BlockSpec(memory_space=pltpu.VMEM),
        scratch_shapes=[
            pltpu.SMEM(a.shape, a.dtype) if n == 3 else pltpu.VMEM(a.shape, a.dtype) for n, a in enumerate(args)
        ]
        + [
            dma((len(args),)),
            pltpu.VMEM((SLABS, SLAB, 128), BF16),
            pltpu.VMEM((SLABS, SLAB, 128), BF16),
            pltpu.VMEM((SLABS, SLAB, 128), BF16),
            pltpu.VMEM((SLABS, SLAB, 128), BF16),
            pltpu.VMEM((2, ENTRIES * 128, 128), BF16),
            pltpu.VMEM((128, 256), BF16),
            pltpu.VMEM((1024, 128), F32),
            pltpu.VMEM((1024, 128), F32),
            pltpu.VMEM((2, 128, 128), BF16),
            pltpu.VMEM((2, 128, 128), BF16),
            pltpu.VMEM((2, 8, 128), F32),
            pltpu.VMEM((2, 8, 128), F32),
            dma(()),
            dma((SIDE,)),
            dma(()),
            dma((SIDE,)),
            dma((2,)),
            dma((2,)),
            dma((4,)),
            dma((4,)),
            pltpu.SemaphoreType.REGULAR,
        ],
        compiler_params=pltpu.CompilerParams(
            collective_id=0, has_side_effects=True, vmem_limit_bytes=32 * 1024 * 1024
        ),
        name="chemistry",
    )(*[pltpu.with_memory_space_constraint(a, pltpu.HBM) for a in args])


def solution(mesh):
    in_specs = (
        P("wide", "narrow", None),
        P("wide", "narrow"),
        P("wide", "narrow", None, None),
        P("wide", "narrow", None),
        P("wide", "narrow", None, None),
        P("wide", "narrow", None, None),
        P("wide", "narrow", None, None, None),
        P("wide", "narrow"),
        P("wide", "narrow"),
        P(),
    )
    out_specs = P("wide", "narrow", None)
    return jax.shard_map(body, mesh=mesh, in_specs=in_specs, out_specs=out_specs, check_vma=False)
```

```python
import jax
import jax.numpy as jnp
from jax import lax
from jax.experimental import pallas as pl
from jax.experimental.pallas import tpu as pltpu
from jax.sharding import PartitionSpec as P

MESH = pl.DeviceIdType.MESH
F32 = jnp.float32
BF16 = jnp.bfloat16

SIDE = 8


def hops(offset):
    return [min(d, SIDE - d) for d in offset]


def longest_first(offset):
    far, (dz, dy) = hops(offset), offset
    return (-sum(far), -max(far), far[0] > far[1], (dz > SIDE // 2) != (dy > SIDE // 2), dz, dy)


OTHERS = sorted([(dz, dy) for dz in range(SIDE) for dy in range(SIDE) if (dz, dy) != (0, 0)], key=longest_first)
NEAR = [o for o in OTHERS if sum(hops(o)) <= 3]
OFFSETS = NEAR + [o for o in OTHERS if o not in NEAR] + [(0, 0)]
NEAR_GROUPS = len(NEAR) // SIDE
COLUMN = [o for o in OTHERS if o[1] == 0]
FIRST = [o for o in OTHERS if o in NEAR or 0 in o]
SELF = len(OFFSETS) - 1
CAP = 12
SLAB = 32
SENT = 26
BACK = 24
ENTRY_ROW = 24
SLABS = 64
GROUP = 8 * SLAB
ENTRIES = 16


def iota(shape, dim):
    return lax.broadcasted_iota(jnp.int32, shape, dim)


def dot(a, b):
    return jnp.dot(a, b, preferred_element_type=F32)


def onehot(match):
    return jnp.where(match, 1.0, 0.0).astype(BF16)


def across(column):
    return jnp.broadcast_to(column, (column.shape[0], 128))


def kernel(
    comps_in, entry_in, dest_in, slots_in, f0_in, x0_in, sens_in, cour_x_in, cour_y_in, diffusion_in, out,
    comps, entry, dest, slots, f0, x0, sens, cour_x, cour_y, diffusion, in_sem,
    send, recv, res, ret, tab_a, tab_xf, col_p, acc, halo_src, halo_dst, edge_src, edge_dst,
    fwd_send, fwd_recv, ret_send, ret_recv, tab_send, tab_recv, halo_send, halo_recv, row_in,
):
    me = lax.axis_index("wide")
    mine_n = lax.axis_index("narrow")
    z, y, c = me // 16, (me // 2) % SIDE, me % 2

    rows_z = [(z + d) % SIDE * 16 for d in range(SIDE)]
    rows_y = [(y + d) % SIDE * 2 + c for d in range(SIDE)]

    def at(dz, dy):
        return {"wide": rows_z[dz % SIDE] + rows_y[dy % SIDE]}

    def behind(a, b):
        dz, dy = OFFSETS[b]
        for g in range(1, SIDE):
            dz = jnp.where(a == g, OFFSETS[g * 8 + b][0], dz)
            dy = jnp.where(a == g, OFFSETS[g * 8 + b][1], dy)
        return {"wide": (z + SIDE - dz) % SIDE * 16 + (y + SIDE - dy) % SIDE * 2 + c}

    def each_group(step, last=SIDE):
        def body(a, carry):
            step(a, SIDE)
            return carry

        lax.fori_loop(0, SIDE - 1, body, 0)
        if last == SIDE:
            step(SIDE - 1, SIDE - 1)

    def remote(src, dst, send_sem, recv_sem, device):
        copy = pltpu.make_async_remote_copy(
            src_ref=src,
            dst_ref=dst,
            send_sem=send_sem,
            recv_sem=recv_sem,
            device_id=device,
            device_id_type=MESH,
        )
        copy.start()
        return copy

    def wait_for(ref, sem):
        pltpu.make_async_copy(ref, ref, sem).wait()

    partner = {"wide": me + 1 - 2 * c}
    above, below = {"wide": (me + 1) % 128}, {"wide": (me + 127) % 128}
    north, south = {"narrow": (mine_n + 1) % 4}, {"narrow": (mine_n + 3) % 4}

    loads = [
        pltpu.make_async_copy(src, dst, in_sem.at[n])
        for n, (src, dst) in enumerate(
            (
                (dest_in, dest),
                (entry_in, entry),
                (comps_in, comps),
                (slots_in, slots),
                (f0_in, f0),
                (x0_in, x0),
                (sens_in, sens),
                (cour_x_in, cour_x),
                (cour_y_in, cour_y),
                (diffusion_in, diffusion),
            )
        )
    ]
    for load in loads:
        load.start()

    recv[...] = jnp.zeros_like(recv)

    barrier = pltpu.get_barrier_semaphore()

    def greet(device):
        pl.semaphore_signal(barrier, inc=1, device_id=device, device_id_type=MESH)

    for offset in FIRST:
        greet(at(*offset))
    for device in (above, below, north, south, partner):
        greet(device)

    ret[...] = jnp.zeros_like(ret)
    tab_xf[pl.ds(32, 96), :] = jnp.zeros((96, 256), BF16)
    for load in loads[:3]:
        load.wait()

    owner = dest[...]
    matches = [iota((128, 128), 0) == owner[i : i + 1, :] for i in range(8)]
    owned = jnp.concatenate([onehot(m) for m in matches], axis=0)
    before = onehot(iota((128, 128), 0) < iota((128, 128), 1))
    counts = dot(owned, jnp.concatenate([before, jnp.ones((128, 128), BF16)], axis=1))
    carry = jnp.zeros((128, 128), F32)
    ranks = []
    for i in range(8):
        part = counts[i * 128 : (i + 1) * 128]
        seen = jnp.where(matches[i], part[:, :128] + carry, 0.0)
        ranks.append(jnp.sum(seen, axis=0, keepdims=True))
        carry = carry + part[:, 128:]
    rank = jnp.concatenate(ranks, axis=0).astype(jnp.int32)

    to_core = owner % 2
    offset = (owner // 16 + SIDE - z) % SIDE * SIDE + (owner // 2 + SIDE - y) % SIDE
    slab = jnp.zeros_like(owner)
    for k, (dz, dy) in enumerate(OFFSETS):
        slab = jnp.where(offset == dz * SIDE + dy, k, slab)
    row = to_core * CAP + rank
    place = slab * SLAB + row
    named = entry[...] + to_core * ENTRIES + 1

    lane = iota((128, 128), 1)
    in_slab = [iota((128, 128), 0) == slab[i : i + 1, :] for i in range(8)]
    in_slab = [jnp.where(m, named[i : i + 1, :].astype(F32), 0.0).astype(BF16) for i, m in enumerate(in_slab)]
    in_row = [onehot(iota((128, 128), 0) == row[i : i + 1, :]) for i in range(8)]
    entry_rows = lax.dot_general(
        jnp.concatenate(in_slab, axis=1),
        jnp.concatenate(in_row, axis=1),
        (((1,), (1,)), ((), ())),
        preferred_element_type=F32,
    ).astype(BF16)
    entry_place = jnp.where(lane[:1] < SLABS, lane[:1] * SLAB + ENTRY_ROW, -1)
    cells = jnp.concatenate([comps[...].reshape(1024, 128), entry_rows], axis=0)
    places = [place[i : i + 1, :] for i in range(8)] + [entry_place]

    def pack(a, carry):
        slot = iota((GROUP, 128), 0) + a * GROUP
        chosen = jnp.concatenate([onehot(slot == p) for p in places], axis=1)
        send[pl.ds(a * 8, 8)] = dot(chosen, cells).astype(BF16).reshape(8, SLAB, 128)
        return carry

    lax.fori_loop(0, NEAR_GROUPS, pack, 0)

    pl.semaphore_wait(barrier, len(FIRST) + 5)

    for offset in COLUMN:
        pl.semaphore_signal(row_in, inc=1, device_id=at(*offset), device_id_type=MESH)

    def send_groups(first, last):
        sent = pl.ds(0, SENT)
        for k in range(first * 8, min(last * 8, SELF)):
            remote(send.at[k, sent], recv.at[k, sent], fwd_send, fwd_recv.at[k // 8], at(*OFFSETS[k]))

    send_groups(0, NEAR_GROUPS)

    for load in loads[3:]:
        load.wait()

    pick = jnp.zeros((ENTRIES, 128), F32)
    for e in range(ENTRIES):
        s = slots[e]
        tab_a[c, pl.ds(e * 128, 128), :] = sens[s]
        pick = jnp.where((iota(pick.shape, 0) == e) & (iota(pick.shape, 1) == s), 1.0, pick)
    xf = jnp.concatenate([x0[...], f0[...]], axis=1)
    xf = jnp.concatenate([xf, jnp.zeros((112, 256), BF16)], axis=0)
    own_rows = pl.ds(pl.multiple_of(c * ENTRIES, ENTRIES), ENTRIES)
    tab_xf[own_rows, :] = dot(pick.astype(BF16), xf).astype(BF16)

    swaps = [
        remote(ref, ref, tab_send.at[n], tab_recv.at[n], partner)
        for n, ref in enumerate((tab_a.at[c], tab_xf.at[own_rows]))
    ]

    lax.fori_loop(NEAR_GROUPS, SIDE, pack, 0)
    recv[SELF] = send[SELF]
    place_t = jnp.transpose(place.astype(F32))
    for i in range(8):
        col_p[pl.ds(i * 128, 128), :] = across(place_t[:, i : i + 1])
    pl.semaphore_wait(row_in, len(COLUMN))
    send_groups(NEAR_GROUPS, SIDE)
    for swap in swaps:
        swap.wait()

    wide_lane = iota((GROUP, 128), 1)
    in_own_row = wide_lane == iota((GROUP, 128), 0) % SLAB
    spread = onehot(iota((GROUP, GROUP), 1) == (iota((GROUP, GROUP), 0) // SLAB) * SLAB + ENTRY_ROW)
    all_ones = jnp.ones((128, 128), BF16)

    def map_group(a, peers):
        wait_for(recv.at[pl.ds(a * 8, peers), pl.ds(0, SENT)], fwd_recv.at[a])
        states = recv[pl.ds(a * 8, 8)].reshape(GROUP, 128)
        named = jnp.where(in_own_row, dot(spread, states), 0.0).astype(BF16)
        named = dot(named, all_ones)
        base = dot(onehot(named == (wide_lane + 1).astype(F32)), tab_xf[...])
        offset = (states.astype(F32) - base[:, :128]).astype(BF16)
        names = named.astype(BF16)
        chosen = [jnp.where(names == jnp.bfloat16(e + 1), offset, jnp.bfloat16(0)) for e in range(2 * ENTRIES)]
        moved = dot(jnp.concatenate(chosen, axis=1), tab_a[...].reshape(2 * ENTRIES * 128, 128))
        res[pl.ds(a * 8, 8)] = (base[:, 128:] + moved).astype(BF16).reshape(8, SLAB, 128)
        for b in range(peers):
            k = a * 8 + b
            back = pl.ds(0, BACK)
            remote(res.at[k, back], ret.at[k, back], ret_send, ret_recv.at[a], behind(a, b))

    each_group(map_group)
    ret[SELF] = res[SELF]

    def chosen_for(a, first, count):
        slot = (iota((count, 128), 1) + a * GROUP).astype(F32)
        at_col = col_p[pl.ds(first, count), :]
        return jnp.concatenate([onehot(at_col == slot), onehot(at_col == slot + 128.0)], axis=1)

    def placed(a, chosen):
        return dot(chosen, ret[pl.ds(a * 8, 8)].reshape(GROUP, 128))

    acc[...] = jnp.zeros_like(acc)

    def place_group(a, peers):
        wait_for(ret.at[pl.ds(a * 8, peers), pl.ds(0, BACK)], ret_recv.at[a])
        acc[...] += placed(a, chosen_for(a, 0, 1024))

    last = SIDE - 1
    each_group(place_group, last)
    outer = [chosen_for(last, first, 128) for first in (0, 896)]
    wait_for(ret.at[pl.ds(last * 8, 7), pl.ds(0, BACK)], ret_recv.at[last])

    def finish(first, count, chosen):
        done = acc[pl.ds(first, count), :] + placed(last, chosen)
        acc[pl.ds(first, count), :] = done
        return done

    def halo(n, src, dst, device):
        return remote(src, dst, halo_send.at[n], halo_recv.at[n], device)

    halo_src[0] = finish(0, 128, outer[0]).astype(BF16)
    halos = [halo(0, halo_src.at[0], halo_dst.at[1], below)]
    halo_src[1] = finish(896, 128, outer[1]).astype(BF16)
    halos.append(halo(1, halo_src.at[1], halo_dst.at[0], above))
    finish(128, 768, chosen_for(last, 128, 768))
    field = [acc[pl.ds(i * 128, 128), :] for i in range(8)]
    edge_src[0] = jnp.concatenate([p[:1] for p in field], axis=0)
    edge_src[1] = jnp.concatenate([p[127:] for p in field], axis=0)
    halos.append(halo(2, edge_src.at[0], edge_dst.at[1], south))
    halos.append(halo(3, edge_src.at[1], edge_dst.at[0], north))

    species = diffusion[...]
    cx_t = jnp.transpose(cour_x[...])
    cy_t = jnp.transpose(cour_y[...])
    nothing = jnp.zeros((128, 128), F32)
    no_row = jnp.zeros((1, 128), F32)
    for i in range(8):
        p = field[i]
        west = field[i - 1] if i > 0 else nothing
        east = field[i + 1] if i < 7 else nothing
        pn = jnp.concatenate([p[1:], no_row], axis=0)
        ps = jnp.concatenate([no_row, p[:127]], axis=0)
        cx, cy = across(cx_t[:, i : i + 1]), across(cy_t[:, i : i + 1])
        r = p - 0.5 * cx * (east - west) + (0.5 * cx * cx + species) * (east - 2.0 * p + west)
        out[i] = r - 0.5 * cy * (pn - ps) + (0.5 * cy * cy + species) * (pn - 2.0 * p + ps)

    for copy in halos:
        copy.wait()

    def weight(courant, sign):
        return sign * 0.5 * courant + 0.5 * courant * courant + species

    low = jnp.where(me > 0, halo_dst[0].astype(F32), 0.0)
    high = jnp.where(me < 127, halo_dst[1].astype(F32), 0.0)
    edge_s = jnp.where(mine_n > 0, edge_dst[0], 0.0)
    edge_n = jnp.where(mine_n < 3, edge_dst[1], 0.0)
    out[0] += low * weight(across(cx_t[:, 0:1]), 1.0)
    out[7] += high * weight(across(cx_t[:, 7:8]), -1.0)
    edge_s = edge_s * weight(across(cour_y[:, 0:1]), 1.0)
    edge_n = edge_n * weight(across(cour_y[:, 127:128]), -1.0)
    for i in range(8):
        out[i, 0:1, :] += edge_s[i : i + 1]
        out[i, 127:128, :] += edge_n[i : i + 1]

    wait_for(send.at[pl.ds(0, SELF), pl.ds(0, SENT)], fwd_send)
    wait_for(res.at[pl.ds(0, SELF), pl.ds(0, BACK)], ret_send)


def body(comps, entry, dest, slot_of_entry, table_f0, table_x0, table_a, courant_x, courant_y, diffusion):
    args = (
        comps,
        entry,
        dest.reshape(entry.shape),
        slot_of_entry.reshape(ENTRIES),
        table_f0[0, 0],
        table_x0[0, 0],
        table_a[0, 0],
        courant_x,
        courant_y,
        diffusion.reshape(1, -1),
    )
    hbm = pl.BlockSpec(memory_space=pltpu.HBM)
    dma = pltpu.SemaphoreType.DMA
    return pl.pallas_call(
        kernel,
        out_shape=jax.ShapeDtypeStruct(comps.shape, F32),
        in_specs=[hbm] * len(args),
        out_specs=pl.BlockSpec(memory_space=pltpu.VMEM),
        scratch_shapes=[
            pltpu.SMEM(a.shape, a.dtype) if n == 3 else pltpu.VMEM(a.shape, a.dtype) for n, a in enumerate(args)
        ]
        + [
            dma((len(args),)),
            pltpu.VMEM((SLABS, SLAB, 128), BF16),
            pltpu.VMEM((SLABS, SLAB, 128), BF16),
            pltpu.VMEM((SLABS, SLAB, 128), BF16),
            pltpu.VMEM((SLABS, SLAB, 128), BF16),
            pltpu.VMEM((2, ENTRIES * 128, 128), BF16),
            pltpu.VMEM((128, 256), BF16),
            pltpu.VMEM((1024, 128), F32),
            pltpu.VMEM((1024, 128), F32),
            pltpu.VMEM((2, 128, 128), BF16),
            pltpu.VMEM((2, 128, 128), BF16),
            pltpu.VMEM((2, 8, 128), F32),
            pltpu.VMEM((2, 8, 128), F32),
            dma(()),
            dma((SIDE,)),
            dma(()),
            dma((SIDE,)),
            dma((2,)),
            dma((2,)),
            dma((4,)),
            dma((4,)),
            pltpu.SemaphoreType.REGULAR,
        ],
        compiler_params=pltpu.CompilerParams(
            collective_id=0, has_side_effects=True, vmem_limit_bytes=32 * 1024 * 1024
        ),
        name="chemistry",
    )(*[pltpu.with_memory_space_constraint(a, pltpu.HBM) for a in args])


def solution(mesh):
    in_specs = (
        P("wide", "narrow", None),
        P("wide", "narrow"),
        P("wide", "narrow", None, None),
        P("wide", "narrow", None),
        P("wide", "narrow", None, None),
        P("wide", "narrow", None, None),
        P("wide", "narrow", None, None, None),
        P("wide", "narrow"),
        P("wide", "narrow"),
        P(),
    )
    out_specs = P("wide", "narrow", None)
    return jax.shard_map(body, mesh=mesh, in_specs=in_specs, out_specs=out_specs, check_vma=False)
```
